128 devices in a mesh: dp: 16 (over z, y_hi, core), mp: 8 (over y_lo, x).
Axes of the slice: x: 4, y: 4 (y_hi: 2, y_lo: 2; y = y_hi * 2 + y_lo), z: 4, core: 2. Of those that a mesh axis runs over, the one named last changes fastest.
Arguments:
- picture_summary_vectors: bfloat16 [16384, 1152], P(('dp', 'mp')), may hold values from -6 to 6
- caption_summary_vectors: bfloat16 [16384, 1152], P(('dp', 'mp')), may hold values from -6 to 6
- picture_mapping_matrix: bfloat16 [1152, 1152], P(('dp', 'mp')), may hold values from -0.1875 to 0.1875
- caption_mapping_matrix: bfloat16 [1152, 1152], P(('dp', 'mp')), may hold values from -0.1875 to 0.1875
- picture_partner_label: int32 [16384], P(('dp', 'mp')), may hold values from 0 to 4095
- caption_partner_label: int32 [16384], P(('dp', 'mp')), may hold values from 0 to 4095
- similarity_factor: float32 [1], replicated, may hold values from 5 to 15
- offset_term: float32 [1], replicated, may hold values from -4 to -1
Outputs:
- img_grad: bfloat16 [16384, 1152], P(('dp', 'mp'))
- txt_grad: bfloat16 [16384, 1152], P(('dp', 'mp'))
- w_img_grad: float32 [1152, 1152], P(('dp', 'mp'))
- w_txt_grad: float32 [1152, 1152], P(('dp', 'mp'))
The draws below stay inside these ranges and needn't reach their ends.
All inputs are finite; a program needn't handle non-finite values.
Results may differ from the reference program's by a relative error of at most 0.023.
Values may be sent and summed in bfloat16 or wider, within the bound.
No kernel may reach another device: no remote copies, remote signals or barrier semaphores. Data moves between devices by JAX's collectives and lax.ppermute only.
A program may use at most 128 MiB of HBM per device.

```python
import math
import jax
import jax.numpy as jnp
from jax import lax

D = 1152
E = 1152
B = 16384


def place_ends(values, own_key, least, top_value):
    index_at = [jax.random.randint(jax.random.fold_in(own_key, axis), (), 0, length) for axis, length in enumerate(values.shape)]
    widest = values.shape.index(max(values.shape))
    neighbour = index_at[:widest] + [(index_at[widest] + 1) % values.shape[widest]] + index_at[widest + 1:]
    return values.at[tuple(index_at)].set(least).at[tuple(neighbour)].set(top_value)


def shard_levels(stream_key, dims, cuts, smallest, top_value):
    level, own = 1.0, jax.random.fold_in(stream_key, 6)
    for dim, blocks in cuts:
        heights = jnp.exp(jax.random.uniform(jax.random.fold_in(own, dim), (blocks,), jnp.float32, smallest / len(cuts), top_value / len(cuts)))
        level = level * jnp.repeat(heights, dims[dim] // blocks).reshape([-1 if axis == dim else 1 for axis in range(len(dims))])
    return level


def normal_values(key, extent, scale, most, cuts=(), held_as=jnp.bfloat16):
    result = jax.random.normal(key, extent, jnp.float32) * scale
    if len(cuts) > 0:
        result = shard_levels(key, extent, cuts, -0.22, 0.18) * result
    return jnp.clip(result, min=-most, max=most).astype(held_as)


def setup_inputs(seed: int = 0) -> dict:
    key_list = jax.random.split(jax.random.key(seed), 9)
    picture_summary_vectors = normal_values(key_list[0], (B, D), 1.0, 6.0, ((0, 128),))
    caption_summary_vectors = normal_values(key_list[1], (B, D), 1.0, 6.0, ((0, 128),))
    picture_mapping_matrix = normal_values(key_list[2], (D, E), D ** -0.5, 0.1875, ((0, 128),))
    caption_mapping_matrix = normal_values(key_list[3], (D, E), D ** -0.5, 0.1875, ((0, 128),))
    picture_partner_label = place_ends(jax.random.randint(key_list[4], (B,), 0, B // 4), jax.random.fold_in(key_list[4], 1), 0, (B // 4) - 1).astype(jnp.int32)
    caption_partner_label = place_ends(jax.random.randint(key_list[5], (B,), 0, B // 4), jax.random.fold_in(key_list[5], 1), 0, (B // 4) - 1).astype(jnp.int32)
    similarity_factor = jnp.clip(jax.random.uniform(key_list[6], (1,), jnp.float32, 5.0, 15.0), 5.0, 15.0)
    offset_term = jnp.clip(jax.random.uniform(key_list[7], (1,), jnp.float32, -4.0, -1.0), -4.0, -1.0)
    return {"picture_summary_vectors": picture_summary_vectors, "caption_summary_vectors": caption_summary_vectors, "picture_mapping_matrix": picture_mapping_matrix, "caption_mapping_matrix": caption_mapping_matrix, "picture_partner_label": picture_partner_label, "caption_partner_label": caption_partner_label, "similarity_factor": similarity_factor, "offset_term": offset_term}


def embed(feat, weight):
    pre = jnp.dot(feat, weight, preferred_element_type=jnp.float32)
    radius = jnp.sqrt(lax.optimization_barrier(jnp.sum(pre * pre, axis=1, keepdims=True)) + 1e-06)
    return (pre / radius, radius)

def backward_rows(unit, radius, grad, feat, weight):
    d_pre = ((grad - unit * lax.optimization_barrier(jnp.sum(unit * grad, axis=1, keepdims=True))) / radius).astype(jnp.bfloat16)
    d_feat = lax.dot_general(d_pre, weight, (((1,), (1,)), ((), ())), preferred_element_type=jnp.float32).astype(jnp.bfloat16)
    d_weight = lax.dot_general(feat, d_pre, (((0,), (0,)), ((), ())), preferred_element_type=jnp.float32)
    return (d_feat, d_weight)

def reference(picture_summary_vectors, caption_summary_vectors, picture_mapping_matrix, caption_mapping_matrix, picture_partner_label, caption_partner_label, similarity_factor, offset_term):
    unit_img, rad_img = embed(picture_summary_vectors, picture_mapping_matrix)
    unit_txt, rad_txt = embed(caption_summary_vectors, caption_mapping_matrix)
    emb_img = unit_img.astype(jnp.bfloat16)
    emb_txt = unit_txt.astype(jnp.bfloat16)
    similarity_multiplier = similarity_factor[0]
    offset = offset_term[0]
    block = math.gcd(B, 1024)
    width = emb_img.shape[1]
    blocks_emb = emb_img.reshape(B // block, block, width)
    blocks_ids = picture_partner_label.reshape(B // block, block)

    def visit(total, item):
        emb_block, ids_block = item
        logits = similarity_multiplier * lax.dot_general(emb_block, emb_txt, (((1,), (1,)), ((), ())), preferred_element_type=jnp.float32) + offset
        sign = jnp.where(ids_block[:, None] == caption_partner_label[None, :], 1.0, -1.0).astype(jnp.float32)
        slope = (-sign * jax.nn.sigmoid(-sign * logits)).astype(jnp.bfloat16)
        image_part = similarity_multiplier * jnp.dot(slope, emb_txt, preferred_element_type=jnp.float32)
        total = total + lax.dot_general(slope, emb_block, (((0,), (0,)), ((), ())), preferred_element_type=jnp.float32)
        return (total, image_part)
    start = jnp.zeros((B, width), jnp.float32)
    total, parts = lax.scan(visit, start, (blocks_emb, blocks_ids))
    d_emb_img = parts.reshape(B, width)
    d_emb_txt = similarity_multiplier * total
    img_grad, w_img_grad = backward_rows(unit_img, rad_img, d_emb_img, picture_summary_vectors, picture_mapping_matrix)
    txt_grad, w_txt_grad = backward_rows(unit_txt, rad_txt, d_emb_txt, caption_summary_vectors, caption_mapping_matrix)
    return (img_grad, txt_grad, w_img_grad, w_txt_grad)
```

```python
import jax
import jax.numpy as jnp
from jax import lax
from jax.experimental import pallas as pl
from jax.experimental.pallas import tpu as pltpu
from jax.sharding import Mesh, PartitionSpec as P

AXES = ("z", "yh", "c", "yl", "x")
CHIPS = ("z", "yh", "yl", "x")
Y = ("yh", "yl")
ROWS = 128
BLOCK = 256
WIDTH = 1152
HALF = 576
STRIP = 81
TEXT_TILE = 512
BF16 = jnp.bfloat16
F32 = jnp.float32


def ring(value, axes, steps):
    count = lax.axis_size(axes)
    return lax.ppermute(value, axes, [(s, (s + steps) % count) for s in range(count)])


def swap(value, axis):
    return lax.ppermute(value, axis, [(0, 1), (1, 0)])


def spread(core):
    wanted = lax.broadcasted_iota(jnp.int32, (WIDTH, HALF), 1)
    wanted = 144 * (wanted // 72) + 72 * core + wanted % 72
    return (lax.broadcasted_iota(jnp.int32, (WIDTH, HALF), 0) == wanted).astype(BF16)


def to_bf16(a, b, dims=((1,), (0,))):
    return lax.dot_general(a, b, (dims, ((), ())), preferred_element_type=F32).astype(BF16)


def gathered(block, axis):
    previous = ring(block, axis, 1)
    following = ring(block, axis, -1)
    far_a = ring(previous[:ROWS], axis, 1)
    far_b = ring(following[ROWS:], axis, -1)
    return [block, following, far_a, far_b, previous]


def reduced(parts, axis):
    own, following, far_a, far_b, previous = parts
    late_a = ring(far_a, axis, -1)
    late_b = ring(far_b, axis, 1)
    previous = jnp.concatenate(
        [(previous[:ROWS].astype(F32) + late_a.astype(F32)).astype(BF16), previous[ROWS:]], 0
    )
    following = jnp.concatenate(
        [following[:ROWS], (following[ROWS:].astype(F32) + late_b.astype(F32)).astype(BF16)], 0
    )
    from_next = ring(previous, axis, -1)
    from_previous = ring(following, axis, 1)
    return own.astype(F32) + from_next.astype(F32) + from_previous.astype(F32)


SIZES = (256, 256, 128, 128, 256)
STARTS = (0, 256, 512, 640, 768)


def pair_kernel(*refs):
    scal, img_ids, txt_ids = refs[:3]
    img_in, txt_in = refs[3:8], refs[8:18]
    img_out, own_out, sib_out = refs[18:23], refs[23], refs[24]
    img, txt, total, sem = refs[25:]
    copies = []
    for k in range(5):
        copies.append(pltpu.make_async_copy(img_in[k], img.at[pl.ds(STARTS[k], SIZES[k])], sem.at[k]))
    for k in range(10):
        at = 1024 * (k // 5) + STARTS[k % 5]
        copies.append(pltpu.make_async_copy(txt_in[k], txt.at[pl.ds(at, SIZES[k % 5])], sem.at[5 + k]))
    for copy in copies:
        copy.start()
    for copy in copies:
        copy.wait()
    factor = scal[0]
    offset = scal[1]
    total[...] = jnp.zeros_like(total)

    def block(step):
        at = pl.multiple_of(step * TEXT_TILE, TEXT_TILE)
        text = txt[pl.ds(at, TEXT_TILE), :]
        logits = lax.dot_general(img[...], text, (((1,), (1,)), ((), ())), preferred_element_type=F32)
        logits = factor * logits + offset
        match = img_ids[...] == txt_ids[:, pl.ds(at, TEXT_TILE)]
        part = 1.0 / (1.0 + jnp.exp(jnp.where(match, logits, -logits)))
        slope = jnp.where(match, -part, part).astype(BF16)
        total[...] += jnp.dot(slope, text, preferred_element_type=F32)
        return lax.dot_general(slope, img[...], (((0,), (0,)), ((), ())), preferred_element_type=F32)

    @pl.loop(0, 2)
    def _(step):
        at = pl.multiple_of(step * TEXT_TILE, TEXT_TILE)
        own_out[pl.ds(at, TEXT_TILE), :] = block(step)

    @pl.loop(0, 2)
    def _(step):
        at = pl.multiple_of(step * TEXT_TILE, TEXT_TILE)
        sib_out[pl.ds(at, TEXT_TILE), :] = block(step + 2).astype(BF16)

    for k in range(5):
        img_out[k][...] = total[pl.ds(STARTS[k], SIZES[k]), :].astype(img_out[k].dtype)


def pairs(scal, img_ids, txt_ids, img, txt):
    vmem = pl.BlockSpec(memory_space=pltpu.VMEM)
    anywhere = pl.BlockSpec(memory_space=pl.ANY)
    out = [jax.ShapeDtypeStruct((n, WIDTH), F32 if k == 0 else BF16) for k, n in enumerate(SIZES)]
    out += [jax.ShapeDtypeStruct((1024, WIDTH), F32), jax.ShapeDtypeStruct((1024, WIDTH), BF16)]
    got = pl.pallas_call(
        pair_kernel,
        out_shape=out,
        in_specs=[pl.BlockSpec(memory_space=pltpu.SMEM), vmem, vmem] + [anywhere] * 15,
        out_specs=[vmem] * 7,
        scratch_shapes=[
            pltpu.VMEM((1024, WIDTH), BF16),
            pltpu.VMEM((2048, WIDTH), BF16),
            pltpu.VMEM((1024, WIDTH), F32),
            pltpu.SemaphoreType.DMA((15,)),
        ],
        compiler_params=pltpu.CompilerParams(vmem_limit_bytes=56 * 1024 * 1024),
        cost_estimate=pl.CostEstimate(flops=3 * 2 * 1024 * 2048 * WIDTH, bytes_accessed=20_000_000, transcendentals=4_000_000),
    )(scal, img_ids, txt_ids, *img, *txt)
    return got[:5], got[5], got[6]


def on_device(img_feat, txt_feat, img_map, txt_map, img_label, txt_label, factor, offset):
    z, yh, c, yl, x = (lax.axis_index(a) for a in AXES)
    is_img = yl == 0
    mine, other = spread(c), spread(1 - c)

    feat = jnp.concatenate([img_feat, txt_feat], 0)
    here = to_bf16(feat, mine)
    there = swap(to_bf16(feat, other), "c")
    nat = lambda v: jnp.where(is_img, v[:ROWS], v[ROWS:])
    alt = lambda v: jnp.where(is_img, v[ROWS:], v[:ROWS])
    moved = swap(jnp.concatenate([alt(here), alt(there)], 0), "yl")
    depth_rows = jnp.concatenate([nat(here), moved[:ROWS], nat(there), moved[ROWS:]], 0)

    labels = jnp.stack([img_label, txt_label])
    coded = jnp.stack([labels // 64, labels % 64], 1).astype(BF16).reshape(4, ROWS)
    both = jnp.stack([img_map.reshape(STRIP, 128), txt_map.reshape(STRIP, 128)])
    both = jnp.concatenate([both, jnp.broadcast_to(coded[None], (2, 4, 128))], 1)
    sent = jnp.broadcast_to(both[None, :, None], (8, 2, 4, STRIP + 4, 128)).reshape(64, STRIP + 4, 128)
    got = lax.all_to_all(sent, CHIPS, 0, 0, tiled=True)
    weight = got[:, :STRIP].reshape(HALF, WIDTH)
    codes = got[:, STRIP:].astype(jnp.int32).reshape(4, 2, 2, 4, 2, 2, ROWS)
    ids = codes[..., 0, :] * 64 + codes[..., 1, :]

    img_set = jnp.where(is_img, yh, 1 - yh)
    img_ids = lax.dynamic_index_in_dim(lax.dynamic_index_in_dim(ids, z, 0, False), img_set, 0, False)
    img_ids = jnp.roll(img_ids[:, :, 0], -x, axis=1).transpose(1, 0, 2).reshape(1024, 1)
    txt_ids = lax.dynamic_index_in_dim(lax.dynamic_index_in_dim(ids, yh, 1, False), x, 2, False)
    txt_ids = jnp.roll(txt_ids[:, ::-1, 1], -z, axis=0).reshape(1, 1024)
    txt_ids = jnp.concatenate([txt_ids, swap(txt_ids, "c")], 1)

    pre = jnp.dot(depth_rows, weight, preferred_element_type=F32)
    pre = pre[:BLOCK] + swap(pre[BLOCK:], "c")
    radius = jnp.sqrt(jnp.sum(pre * pre, axis=1, keepdims=True) + 1e-06)
    unit = pre / radius
    emb = unit.astype(BF16)

    shifted = ring(emb, Y, -1)
    img = gathered(jnp.where(is_img, emb, shifted), "x")
    txt = gathered(jnp.where(is_img, shifted, emb), "z")
    txt = txt + [swap(v, "c") for v in txt]

    scal = jnp.concatenate([factor, offset])
    img_parts, own, sib = pairs(scal, img_ids, txt_ids, img, txt)

    added = swap(sib, "c")
    txt_parts = []
    for k in range(5):
        span = slice(STARTS[k], STARTS[k] + SIZES[k])
        part = own[span] + added[span].astype(F32)
        txt_parts.append(part if k == 0 else part.astype(BF16))
    d_img = reduced(img_parts, "x")
    d_txt = reduced(txt_parts, "z")
    back = ring(jnp.where(is_img, d_txt, d_img).astype(BF16), Y, 1)
    grad = factor[0] * (jnp.where(is_img, d_img, d_txt) + back.astype(F32))

    d_pre = ((grad - unit * jnp.sum(unit * grad, axis=1, keepdims=True)) / radius).astype(BF16)
    d_pre = jnp.concatenate([d_pre, swap(d_pre, "c")], 0)
    d_weight = to_bf16(depth_rows, d_pre, ((0,), (0,)))
    d_weight = lax.all_to_all(d_weight.reshape(64, STRIP, 128), CHIPS, 0, 0, tiled=True)
    d_weight = jnp.sum(d_weight.reshape(8, 2, 4, STRIP, 128).astype(F32), axis=(0, 2))
    d_weight = d_weight.reshape(2, 9, WIDTH)

    d_feat = to_bf16(d_pre, weight, ((1,), (1,)))
    moved = swap(jnp.concatenate([d_feat[ROWS:BLOCK], d_feat[BLOCK + ROWS :]], 0), "yl")
    here = jnp.concatenate([d_feat[:ROWS], moved[:ROWS]], 0)
    there = swap(jnp.concatenate([d_feat[BLOCK : BLOCK + ROWS], moved[ROWS:]], 0), "c")
    d_rows = to_bf16(
        jnp.concatenate([here, there], 1), jnp.concatenate([mine, other], 1), ((1,), (1,))
    )
    nat_grad, alt_grad = d_rows[:ROWS], d_rows[ROWS:]
    img_grad = jnp.where(is_img, nat_grad, alt_grad)
    txt_grad = jnp.where(is_img, alt_grad, nat_grad)
    return (img_grad, txt_grad, d_weight[0], d_weight[1])


def solution(mesh):
    fine = Mesh(mesh.devices.reshape(4, 2, 2, 2, 4), AXES)
    rows = P(AXES, None)
    return jax.shard_map(
        on_device,
        mesh=fine,
        in_specs=(rows, rows, rows, rows, P(AXES), P(AXES), P(), P()),
        out_specs=(rows, rows, rows, rows),
        check_vma=False,
    )
```

```python
import functools

import jax
import jax.numpy as jnp
from jax import lax
from jax.experimental import pallas as pl
from jax.experimental.pallas import tpu as pltpu
from jax.sharding import Mesh, PartitionSpec as P

AXES = ("z", "yh", "c", "yl", "x")
CHIPS = ("z", "yh", "yl", "x")
Y = ("yh", "yl")
ROWS = 128
BLOCK = 256
WIDTH = 1152
HALF = 576
STRIP = 81
BF16 = jnp.bfloat16
F32 = jnp.float32


def ring(value, axes, steps):
    count = lax.axis_size(axes)
    return lax.ppermute(value, axes, [(s, (s + steps) % count) for s in range(count)])


def swap(value, axis):
    return lax.ppermute(value, axis, [(0, 1), (1, 0)])


def spread(core):
    wanted = lax.broadcasted_iota(jnp.int32, (WIDTH, HALF), 1)
    wanted = 144 * (wanted // 72) + 72 * core + wanted % 72
    return (lax.broadcasted_iota(jnp.int32, (WIDTH, HALF), 0) == wanted).astype(BF16)


def to_bf16(a, b, dims=((1,), (0,))):
    return lax.dot_general(a, b, (dims, ((), ())), preferred_element_type=F32).astype(BF16)


def ring_pairs(steps, native):
    pairs = []
    for z in range(4):
        for yl in range(2):
            for x in range(4):
                along_x = (yl == 0) == native
                to = (z, (x + steps) % 4) if along_x else ((z + steps) % 4, x)
                pairs.append(((z * 2 + yl) * 4 + x, (to[0] * 2 + yl) * 4 + to[1]))
    return pairs


def step(value, steps, native):
    return lax.ppermute(value, ("z", "yl", "x"), ring_pairs(steps, native))


def gathered(block, native):
    previous = step(block, 1, native)
    following = step(block, -1, native)
    far_a = step(previous[:ROWS], 1, native)
    far_b = step(following[ROWS:], -1, native)
    return [block, following, far_a, far_b, previous]


def added_half(whole, half, first):
    low, high = whole[:ROWS], whole[ROWS:]
    if first:
        low = (low.astype(F32) + half.astype(F32)).astype(BF16)
    else:
        high = (high.astype(F32) + half.astype(F32)).astype(BF16)
    return jnp.concatenate([low, high], 0)


def reduced(parts, native):
    own, following, far_a, far_b, previous = parts
    late_a = step(far_a, -1, native)
    late_b = step(far_b, 1, native)
    from_next = step(added_half(previous, late_a, True), -1, native)
    from_previous = step(added_half(following, late_b, False), 1, native)
    return own.astype(F32) + from_next.astype(F32) + from_previous.astype(F32)


SIZES = (256, 256, 128, 128, 256)
STARTS = (0, 256, 512, 640, 768)
TILE = 256
VMEM = pl.BlockSpec(memory_space=pltpu.VMEM)
ANYWHERE = pl.BlockSpec(memory_space=pl.ANY)


def slope_kernel(sizes, *refs):
    count = len(sizes)
    scal, row_ids, nat_ids = refs[:3]
    row_in, nat_in = refs[3 : 3 + count], refs[3 + count : 13 + count]
    slopes = refs[13 + count]
    sums = refs[14 + count : 14 + 2 * count]
    rows, nat, total, sem = refs[14 + 2 * count :]
    copies, start = [], 0
    for k, size in enumerate(sizes):
        copies.append(pltpu.make_async_copy(row_in[k], rows.at[pl.ds(start, size)], sem.at[10 + k]))
        start += size
    nat_copies = [
        pltpu.make_async_copy(
            nat_in[k], nat.at[pl.ds(1024 * (k // 5) + STARTS[k % 5], SIZES[k % 5])], sem.at[k]
        )
        for k in range(10)
    ]
    for copy in copies + nat_copies:
        copy.start()
    for copy in copies:
        copy.wait()
    factor = scal[0]
    offset = scal[1]
    needed = ((0,), (1,), (2, 3), (4,), (5,), (6,), (7, 8), (9,))

    def logits(tile):
        for k in needed[tile]:
            nat_copies[k].wait()
        return lax.dot_general(
            rows[...], nat[pl.ds(tile * TILE, TILE), :], (((1,), (1,)), ((), ())), preferred_element_type=F32
        )

    following = logits(0)
    for tile in range(8):
        current = following
        if tile < 7:
            following = logits(tile + 1)
        current = factor * current + offset
        match = row_ids[...] == nat_ids[:, pl.ds(tile * TILE, TILE)]
        part = 1.0 / (1.0 + jnp.exp(jnp.where(match, current, -current)))
        slope = jnp.where(match, -part, part).astype(BF16)
        slopes[:, pl.ds(tile * TILE, TILE)] = slope
        term = jnp.dot(slope, nat[pl.ds(tile * TILE, TILE), :], preferred_element_type=F32)
        if tile == 0:
            total[...] = term
        else:
            total[...] += term
    start = 0
    for k, size in enumerate(sizes):
        sums[k][...] = total[pl.ds(start, size), :].astype(sums[k].dtype)
        start += size


def slopes_of(scal, row_ids, nat_ids, rows, nat, dtype):
    sizes = tuple(r.shape[0] for r in rows)
    whole = sum(sizes)
    got = pl.pallas_call(
        functools.partial(slope_kernel, sizes),
        out_shape=[jax.ShapeDtypeStruct((whole, 2048), BF16)]
        + [jax.ShapeDtypeStruct((n, WIDTH), dtype) for n in sizes],
        in_specs=[pl.BlockSpec(memory_space=pltpu.SMEM), VMEM, VMEM] + [ANYWHERE] * (len(sizes) + 10),
        out_specs=[VMEM] * (1 + len(sizes)),
        scratch_shapes=[
            pltpu.VMEM((whole, WIDTH), BF16),
            pltpu.VMEM((2048, WIDTH), BF16),
            pltpu.VMEM((whole, WIDTH), F32),
            pltpu.SemaphoreType.DMA((10 + len(sizes),)),
        ],
        compiler_params=pltpu.CompilerParams(vmem_limit_bytes=40 * 1024 * 1024),
        cost_estimate=pl.CostEstimate(
            flops=4 * whole * 2048 * WIDTH, bytes_accessed=8_000_000, transcendentals=2 * whole * 2048
        ),
    )(scal, row_ids, nat_ids, *rows, *nat)
    return got[0], got[1:]


def nat_kernel(*refs):
    slopes, row_in, out = refs[:3], refs[3:8], refs[8]
    starts = (0, 256, 512, 640, 768)
    which = ((0,), (1, 4), (2, 3))

    for tile in range(1024 // TILE):
        at = pl.ds(tile * TILE, TILE)
        total = None
        for group, members in zip(slopes, which):
            start = 0
            for k in members:
                size = row_in[k].shape[0]
                term = lax.dot_general(
                    group[pl.ds(start, size), at], row_in[k][...], (((0,), (0,)), ((), ())), preferred_element_type=F32
                )
                total = term if total is None else total + term
                start += size
        out[at, :] = total.astype(out.dtype)


def nat_sums(slopes, rows, part, dtype):
    specs = [pl.BlockSpec((s.shape[0], 1024), lambda i: (0, part), memory_space=pltpu.VMEM) for s in slopes]
    specs += [pl.BlockSpec(r.shape, lambda i: (0, 0), memory_space=pltpu.VMEM) for r in rows]
    return pl.pallas_call(
        nat_kernel,
        grid=(1,),
        out_shape=jax.ShapeDtypeStruct((1024, WIDTH), dtype),
        in_specs=specs,
        out_specs=pl.BlockSpec((1024, WIDTH), lambda i: (0, 0), memory_space=pltpu.VMEM),
        compiler_params=pltpu.CompilerParams(vmem_limit_bytes=40 * 1024 * 1024),
        cost_estimate=pl.CostEstimate(
            flops=2 * 1024 * 1024 * WIDTH, bytes_accessed=8_000_000, transcendentals=0
        ),
    )(*slopes, *rows)


def on_device(img_feat, txt_feat, img_map, txt_map, img_label, txt_label, factor, offset):
    z, yh, c, yl, x = (lax.axis_index(a) for a in AXES)
    is_img = yl == 0
    mine, other = spread(c), spread(1 - c)

    feat = jnp.concatenate([img_feat, txt_feat], 0)
    here = to_bf16(feat, mine)
    there = swap(to_bf16(feat, other), "c")
    nat = lambda v: jnp.where(is_img, v[:ROWS], v[ROWS:])
    alt = lambda v: jnp.where(is_img, v[ROWS:], v[:ROWS])
    moved = swap(jnp.concatenate([alt(here), alt(there)], 0), "yl")
    depth_rows = jnp.concatenate([nat(here), moved[:ROWS], nat(there), moved[ROWS:]], 0)

    labels = jnp.stack([img_label, txt_label])
    coded = jnp.stack([labels // 64, labels % 64], 1).astype(BF16).reshape(4, ROWS)
    both = jnp.stack([img_map.reshape(STRIP, 128), txt_map.reshape(STRIP, 128)])
    both = jnp.concatenate([both, jnp.broadcast_to(coded[None], (2, 4, 128)), jnp.zeros((2, 3, 128), BF16)], 1)
    sent = jnp.broadcast_to(both[None, :, None], (8, 2, 4, STRIP + 7, 128)).reshape(64, STRIP + 7, 128)
    got = lax.all_to_all(sent, CHIPS, 0, 0, tiled=True)
    weight = got[:, :STRIP].reshape(HALF, WIDTH)
    codes = got[:, STRIP : STRIP + 4].astype(jnp.int32).reshape(4, 2, 2, 4, 2, 2, ROWS)
    ids = codes[..., 0, :] * 64 + codes[..., 1, :]

    def img_ids(pair):
        got = lax.dynamic_index_in_dim(lax.dynamic_index_in_dim(ids, z, 0, False), pair, 0, False)
        return jnp.roll(got[:, :, 0], -x, axis=1).transpose(1, 0, 2).reshape(1024)

    txt_ids = lax.dynamic_index_in_dim(lax.dynamic_index_in_dim(ids, yh, 1, False), x, 2, False)
    txt_ids = jnp.roll(txt_ids[:, ::-1, 1], -z, axis=0).reshape(1024)
    nat_ids = jnp.where(is_img, img_ids(yh), txt_ids).reshape(1, 1024)
    nat_ids = jnp.concatenate([nat_ids, swap(nat_ids, "c")], 1)
    row_ids = jnp.where(is_img, txt_ids, img_ids(1 - yh)).reshape(1024, 1)

    pre = jnp.dot(depth_rows, weight, preferred_element_type=F32)
    pre = pre[:BLOCK] + swap(pre[BLOCK:], "c")
    radius = jnp.sqrt(jnp.sum(pre * pre, axis=1, keepdims=True) + 1e-06)
    unit = pre / radius
    emb = unit.astype(BF16)

    moved = ring(emb, Y, -1)
    nat = gathered(emb, True)
    nat = nat + [swap(v, "c") for v in nat]
    rows = gathered(moved, False)

    scal = jnp.concatenate([factor, offset])
    slope_own, (sum_own,) = slopes_of(scal, row_ids[:256], nat_ids, [rows[0]], nat, F32)
    beside_ids = jnp.concatenate([row_ids[256:512], row_ids[768:]], 0)
    slope_beside, (sum_next, sum_previous) = slopes_of(scal, beside_ids, nat_ids, [rows[1], rows[4]], nat, BF16)
    slope_far, (sum_a, sum_b) = slopes_of(scal, row_ids[512:768], nat_ids, [rows[2], rows[3]], nat, BF16)
    slopes = (slope_own, slope_beside, slope_far)
    sib = nat_sums(slopes, rows, 1, BF16)
    own = nat_sums(slopes, rows, 0, F32)

    added = swap(sib, "c")
    nat_parts = []
    for k in range(5):
        span = slice(STARTS[k], STARTS[k] + SIZES[k])
        part = own[span] + added[span].astype(F32)
        nat_parts.append(part if k == 0 else part.astype(BF16))
    d_moved = reduced([sum_own, sum_next, sum_a, sum_b, sum_previous], False)
    back = ring(d_moved.astype(BF16), Y, 1)
    d_nat = reduced(nat_parts, True)
    grad = factor[0] * (d_nat + back.astype(F32))

    d_pre = ((grad - unit * jnp.sum(unit * grad, axis=1, keepdims=True)) / radius).astype(BF16)
    d_pre = jnp.concatenate([d_pre, swap(d_pre, "c")], 0)
    d_weight = to_bf16(depth_rows, d_pre, ((0,), (0,)))
    d_weight = lax.all_to_all(d_weight.reshape(64, STRIP, 128), CHIPS, 0, 0, tiled=True)
    d_weight = jnp.sum(d_weight.reshape(8, 2, 4, STRIP, 128).astype(F32), axis=(0, 2))
    d_weight = d_weight.reshape(2, 9, WIDTH)

    d_feat = to_bf16(d_pre, weight, ((1,), (1,)))
    moved = swap(jnp.concatenate([d_feat[ROWS:BLOCK], d_feat[BLOCK + ROWS :]], 0), "yl")
    here = jnp.concatenate([d_feat[:ROWS], moved[:ROWS]], 0)
    there = swap(jnp.concatenate([d_feat[BLOCK : BLOCK + ROWS], moved[ROWS:]], 0), "c")
    d_rows = to_bf16(
        jnp.concatenate([here, there], 1), jnp.concatenate([mine, other], 1), ((1,), (1,))
    )
    nat_grad, alt_grad = d_rows[:ROWS], d_rows[ROWS:]
    img_grad = jnp.where(is_img, nat_grad, alt_grad)
    txt_grad = jnp.where(is_img, alt_grad, nat_grad)
    return (img_grad, txt_grad, d_weight[0], d_weight[1])


def solution(mesh):
    fine = Mesh(mesh.devices.reshape(4, 2, 2, 2, 4), AXES)
    rows = P(AXES, None)
    return jax.shard_map(
        on_device,
        mesh=fine,
        in_specs=(rows, rows, rows, rows, P(AXES), P(AXES), P(), P()),
        out_specs=(rows, rows, rows, rows),
        check_vma=False,
    )
```

```python
import functools

import jax
import jax.numpy as jnp
from jax import lax
from jax.experimental import pallas as pl
from jax.experimental.pallas import tpu as pltpu
from jax.sharding import Mesh, PartitionSpec as P

AXES = ("z", "yh", "c", "yl", "x")
CHIPS = ("z", "yh", "yl", "x")
Y = ("yh", "yl")
ROWS = 128
BLOCK = 256
WIDTH = 1152
HALF = 576
STRIP = 81
BF16 = jnp.bfloat16
F32 = jnp.float32


def ring(value, axes, steps):
    count = lax.axis_size(axes)
    return lax.ppermute(value, axes, [(s, (s + steps) % count) for s in range(count)])


def swap(value, axis):
    return lax.ppermute(value, axis, [(0, 1), (1, 0)])


def spread(core):
    wanted = lax.broadcasted_iota(jnp.int32, (WIDTH, HALF), 1)
    wanted = 144 * (wanted // 72) + 72 * core + wanted % 72
    return (lax.broadcasted_iota(jnp.int32, (WIDTH, HALF), 0) == wanted).astype(BF16)


def to_bf16(a, b, dims=((1,), (0,))):
    return lax.dot_general(a, b, (dims, ((), ())), preferred_element_type=F32).astype(BF16)


def ring_pairs(steps, native):
    pairs = []
    for z in range(4):
        for yl in range(2):
            for x in range(4):
                along_x = (yl == 0) == native
                to = (z, (x + steps) % 4) if along_x else ((z + steps) % 4, x)
                pairs.append(((z * 2 + yl) * 4 + x, (to[0] * 2 + yl) * 4 + to[1]))
    return pairs


def step(value, steps, native):
    return lax.ppermute(value, ("z", "yl", "x"), ring_pairs(steps, native))


def gathered(block, native):
    previous = step(block, 1, native)
    following = step(block, -1, native)
    far_a = step(previous[:ROWS], 1, native)
    far_b = step(following[ROWS:], -1, native)
    return [block, following, far_a, far_b, previous]


def added_half(whole, half, first):
    low, high = whole[:ROWS], whole[ROWS:]
    if first:
        low = (low.astype(F32) + half.astype(F32)).astype(BF16)
    else:
        high = (high.astype(F32) + half.astype(F32)).astype(BF16)
    return jnp.concatenate([low, high], 0)


def reduced(parts, native):
    own, following, far_a, far_b, previous = parts
    late_a = step(far_a, -1, native)
    late_b = step(far_b, 1, native)
    from_next = step(added_half(previous, late_a, True), -1, native)
    from_previous = step(added_half(following, late_b, False), 1, native)
    return own.astype(F32) + from_next.astype(F32) + from_previous.astype(F32)


SIZES = (256, 256, 128, 128, 256)
STARTS = (0, 256, 512, 640, 768)
TILE = 256
VMEM = pl.BlockSpec(memory_space=pltpu.VMEM)
ANYWHERE = pl.BlockSpec(memory_space=pl.ANY)


def slope_kernel(sizes, waits, *refs):
    count = len(sizes)
    scal, row_ids, nat_ids = refs[:3]
    row_in, nat_in = refs[3 : 3 + count], refs[3 + count : 13 + count]
    outs = refs[13 + count + waits :]
    slopes, sums = outs[0], outs[1 : 1 + count]
    rows, total = outs[1 + count :]
    start = 0
    for k, size in enumerate(sizes):
        rows[pl.ds(start, size), :] = row_in[k][...]
        start += size
    factor = scal[0]
    offset = scal[1]
    tiles = [(1024 * (k // 5) + STARTS[k % 5], SIZES[k % 5], nat_in[k]) for k in range(10)]

    def logits(tile):
        return lax.dot_general(
            rows[...], tiles[tile][2][...], (((1,), (1,)), ((), ())), preferred_element_type=F32
        )

    following = logits(0)
    for tile, (at, size, nat) in enumerate(tiles):
        current = following
        if tile < 9:
            following = logits(tile + 1)
        current = factor * current + offset
        match = row_ids[...] == nat_ids[:, pl.ds(at, size)]
        part = 1.0 / (1.0 + jnp.exp(jnp.where(match, current, -current)))
        slope = jnp.where(match, -part, part).astype(BF16)
        slopes[:, pl.ds(at, size)] = slope
        term = jnp.dot(slope, nat[...], preferred_element_type=F32)
        if tile == 0:
            total[...] = term
        else:
            total[...] += term
    start = 0
    for k, size in enumerate(sizes):
        sums[k][...] = total[pl.ds(start, size), :].astype(sums[k].dtype)
        start += size


def slopes_of(scal, row_ids, nat_ids, rows, nat, dtype, after=()):
    sizes = tuple(r.shape[0] for r in rows)
    whole = sum(sizes)
    got = pl.pallas_call(
        functools.partial(slope_kernel, sizes, len(after)),
        out_shape=[jax.ShapeDtypeStruct((whole, 2048), BF16)]
        + [jax.ShapeDtypeStruct((n, WIDTH), dtype) for n in sizes],
        in_specs=[pl.BlockSpec(memory_space=pltpu.SMEM)] + [VMEM] * (len(sizes) + 12) + [ANYWHERE] * len(after),
        out_specs=[VMEM] * (1 + len(sizes)),
        scratch_shapes=[pltpu.VMEM((whole, WIDTH), BF16), pltpu.VMEM((whole, WIDTH), F32)],
        compiler_params=pltpu.CompilerParams(vmem_limit_bytes=40 * 1024 * 1024),
        cost_estimate=pl.CostEstimate(
            flops=4 * whole * 2048 * WIDTH, bytes_accessed=8_000_000, transcendentals=2 * whole * 2048
        ),
    )(scal, row_ids, nat_ids, *rows, *nat, *after)
    return got[0], got[1:]


def nat_kernel(part, *refs):
    slopes, row_in, far, near = refs[:3], refs[3:8], refs[8], refs[9]
    which = ((0,), (1, 4), (2, 3))
    places = {512: (far, 0), 0: (near, 0), 256: (near, 256), 768: (near, 512)}
    for begin in (512, 0, 256, 768):
        total = None
        for group, members in zip(slopes, which):
            start = 0
            for k in members:
                size = row_in[k].shape[0]
                term = lax.dot_general(
                    group[pl.ds(start, size), pl.ds(1024 * part + begin, TILE)],
                    row_in[k][...],
                    (((0,), (0,)), ((), ())),
                    preferred_element_type=F32,
                )
                total = term if total is None else total + term
                start += size
        out, at = places[begin]
        out[pl.ds(at, TILE), :] = total.astype(out.dtype)


def nat_sums(slopes, rows, part, dtype, after=()):
    return pl.pallas_call(
        lambda *refs: nat_kernel(part, *refs[:8], *refs[8 + len(after) :]),
        out_shape=[jax.ShapeDtypeStruct((n, WIDTH), dtype) for n in (256, 768)],
        in_specs=[VMEM] * 8 + [ANYWHERE] * len(after),
        out_specs=[VMEM] * 2,
        compiler_params=pltpu.CompilerParams(vmem_limit_bytes=40 * 1024 * 1024),
        cost_estimate=pl.CostEstimate(
            flops=2 * 1024 * 1024 * WIDTH, bytes_accessed=8_000_000, transcendentals=0
        ),
    )(*slopes, *rows, *after)


def on_device(img_feat, txt_feat, img_map, txt_map, img_label, txt_label, factor, offset):
    z, yh, c, yl, x = (lax.axis_index(a) for a in AXES)
    is_img = yl == 0
    mine, other = spread(c), spread(1 - c)

    feat = jnp.concatenate([img_feat, txt_feat], 0)
    here = to_bf16(feat, mine)
    there = swap(to_bf16(feat, other), "c")
    nat = lambda v: jnp.where(is_img, v[:ROWS], v[ROWS:])
    alt = lambda v: jnp.where(is_img, v[ROWS:], v[:ROWS])
    moved = swap(jnp.concatenate([alt(here), alt(there)], 0), "yl")
    depth_rows = jnp.concatenate([nat(here), moved[:ROWS], nat(there), moved[ROWS:]], 0)

    labels = jnp.stack([img_label, txt_label])
    coded = jnp.stack([labels // 64, labels % 64], 1).astype(BF16).reshape(4, ROWS)
    both = jnp.stack([img_map.reshape(STRIP, 128), txt_map.reshape(STRIP, 128)])
    both = jnp.concatenate([both, jnp.broadcast_to(coded[None], (2, 4, 128)), jnp.zeros((2, 3, 128), BF16)], 1)
    sent = jnp.broadcast_to(both[None, :, None], (8, 2, 4, STRIP + 7, 128)).reshape(64, STRIP + 7, 128)
    got = lax.all_to_all(sent, CHIPS, 0, 0, tiled=True)
    weight = got[:, :STRIP].reshape(HALF, WIDTH)
    codes = got[:, STRIP : STRIP + 4].astype(jnp.int32).reshape(4, 2, 2, 4, 2, 2, ROWS)
    ids = codes[..., 0, :] * 64 + codes[..., 1, :]

    def img_ids(pair):
        got = lax.dynamic_index_in_dim(lax.dynamic_index_in_dim(ids, z, 0, False), pair, 0, False)
        return jnp.roll(got[:, :, 0], -x, axis=1).transpose(1, 0, 2).reshape(1024)

    txt_ids = lax.dynamic_index_in_dim(lax.dynamic_index_in_dim(ids, yh, 1, False), x, 2, False)
    txt_ids = jnp.roll(txt_ids[:, ::-1, 1], -z, axis=0).reshape(1024)
    nat_ids = jnp.where(is_img, img_ids(yh), txt_ids).reshape(1, 1024)
    nat_ids = jnp.concatenate([nat_ids, swap(nat_ids, "c")], 1)
    row_ids = jnp.where(is_img, txt_ids, img_ids(1 - yh)).reshape(1024, 1)

    pre = jnp.dot(depth_rows, weight, preferred_element_type=F32)
    pre = pre[:BLOCK] + swap(pre[BLOCK:], "c")
    radius = jnp.sqrt(jnp.sum(pre * pre, axis=1, keepdims=True) + 1e-06)
    unit = pre / radius
    emb = unit.astype(BF16)

    moved = ring(emb, Y, -1)
    nat = gathered(emb, True)
    nat = nat + [swap(v, "c") for v in nat]
    rows = gathered(moved, False)

    scal = jnp.concatenate([factor, offset])
    slope_own, (sum_own,) = slopes_of(scal, row_ids[:256], nat_ids, [rows[0]], nat, F32)
    beside_ids = jnp.concatenate([row_ids[256:512], row_ids[768:]], 0)
    slope_beside, (sum_next, sum_previous) = slopes_of(scal, beside_ids, nat_ids, [rows[1], rows[4]], nat, BF16, (slope_own,))
    slope_far, (sum_a, sum_b) = slopes_of(scal, row_ids[512:768], nat_ids, [rows[2], rows[3]], nat, BF16, (slope_own,))
    slopes = (slope_own, slope_beside, slope_far)
    sib_far, sib_near = nat_sums(slopes, rows, 1, BF16)
    own_far, own_near = nat_sums(slopes, rows, 0, F32, (sib_far,))
    far = (own_far + swap(sib_far, "c").astype(F32)).astype(BF16)
    sib_near = swap(sib_near, "c").astype(F32)
    near = [own_near[at : at + 256] + sib_near[at : at + 256] for at in (0, 256, 512)]
    nat_parts = [near[0], near[1].astype(BF16), far[:ROWS], far[ROWS:], near[2].astype(BF16)]
    d_moved = reduced([sum_own, sum_next, sum_a, sum_b, sum_previous], False)
    back = ring(d_moved.astype(BF16), Y, 1)
    d_nat = reduced(nat_parts, True)
    grad = factor[0] * (d_nat + back.astype(F32))

    d_pre = ((grad - unit * jnp.sum(unit * grad, axis=1, keepdims=True)) / radius).astype(BF16)
    d_pre = jnp.concatenate([d_pre, swap(d_pre, "c")], 0)
    d_weight = to_bf16(depth_rows, d_pre, ((0,), (0,)))
    d_weight = lax.all_to_all(d_weight.reshape(64, STRIP, 128), CHIPS, 0, 0, tiled=True)
    d_weight = jnp.sum(d_weight.reshape(8, 2, 4, STRIP, 128).astype(F32), axis=(0, 2))
    d_weight = d_weight.reshape(2, 9, WIDTH)

    d_feat = to_bf16(d_pre, weight, ((1,), (1,)))
    moved = swap(jnp.concatenate([d_feat[ROWS:BLOCK], d_feat[BLOCK + ROWS :]], 0), "yl")
    here = jnp.concatenate([d_feat[:ROWS], moved[:ROWS]], 0)
    there = swap(jnp.concatenate([d_feat[BLOCK : BLOCK + ROWS], moved[ROWS:]], 0), "c")
    d_rows = to_bf16(
        jnp.concatenate([here, there], 1), jnp.concatenate([mine, other], 1), ((1,), (1,))
    )
    nat_grad, alt_grad = d_rows[:ROWS], d_rows[ROWS:]
    img_grad = jnp.where(is_img, nat_grad, alt_grad)
    txt_grad = jnp.where(is_img, alt_grad, nat_grad)
    return (img_grad, txt_grad, d_weight[0], d_weight[1])


def solution(mesh):
    fine = Mesh(mesh.devices.reshape(4, 2, 2, 2, 4), AXES)
    rows = P(AXES, None)
    return jax.shard_map(
        on_device,
        mesh=fine,
        in_specs=(rows, rows, rows, rows, P(AXES), P(AXES), P(), P()),
        out_specs=(rows, rows, rows, rows),
        check_vma=False,
    )
```

```python
import functools

import jax
import jax.numpy as jnp
from jax import lax
from jax.experimental import pallas as pl
from jax.experimental.pallas import tpu as pltpu
from jax.sharding import Mesh, PartitionSpec as P

AXES = ("z", "yh", "c", "yl", "x")
CHIPS = ("z", "yh", "yl", "x")
Y = ("yh", "yl")
ROWS = 128
BLOCK = 256
WIDTH = 1152
HALF = 576
STRIP = 81
BF16 = jnp.bfloat16
F32 = jnp.float32


def ring(value, axes, steps):
    count = lax.axis_size(axes)
    return lax.ppermute(value, axes, [(s, (s + steps) % count) for s in range(count)])


def swap(value, axis):
    return lax.ppermute(value, axis, [(0, 1), (1, 0)])


def spread(core):
    wanted = lax.broadcasted_iota(jnp.int32, (WIDTH, HALF), 1)
    wanted = 144 * (wanted // 72) + 72 * core + wanted % 72
    return (lax.broadcasted_iota(jnp.int32, (WIDTH, HALF), 0) == wanted).astype(BF16)


def to_bf16(a, b, dims=((1,), (0,))):
    return lax.dot_general(a, b, (dims, ((), ())), preferred_element_type=F32).astype(BF16)


def ring_pairs(steps, native):
    pairs = []
    for z in range(4):
        for yl in range(2):
            for x in range(4):
                along_x = (yl == 0) == native
                to = (z, (x + steps) % 4) if along_x else ((z + steps) % 4, x)
                pairs.append(((z * 2 + yl) * 4 + x, (to[0] * 2 + yl) * 4 + to[1]))
    return pairs


def step(value, steps, native):
    return lax.ppermute(value, ("z", "yl", "x"), ring_pairs(steps, native))


def gathered(block, native):
    previous = step(block, 1, native)
    following = step(block, -1, native)
    far_a = step(previous[:ROWS], 1, native)
    far_b = step(following[ROWS:], -1, native)
    return [block, following, far_a, far_b, previous]


def added_half(whole, half, first):
    low, high = whole[:ROWS], whole[ROWS:]
    if first:
        low = (low.astype(F32) + half.astype(F32)).astype(BF16)
    else:
        high = (high.astype(F32) + half.astype(F32)).astype(BF16)
    return jnp.concatenate([low, high], 0)


def reduced(parts, native, first=None):
    own, following, far_a, far_b, previous = parts
    late = step(far_a, -1, native), step(far_b, 1, native)
    if first is not None:
        late = lax.optimization_barrier((*late, *first))
    previous = added_half(previous, late[0], True)
    following = added_half(following, late[1], False)
    from_next = step(previous, -1, native)
    from_previous = step(following, 1, native)
    return own.astype(F32) + from_next.astype(F32) + from_previous.astype(F32), (previous, following)


TILE = 256
SCOPED = 13 * 1024 * 1024
LOG2_E = 1.4426950408889634
VMEM = pl.BlockSpec(memory_space=pltpu.VMEM)
ANYWHERE = pl.BlockSpec(memory_space=pl.ANY)


def id_row(places, codes, native, along, half):
    z, yh, yl, x = (places[k] for k in range(4))
    pair = yh if native else jnp.where(yl == 0, yh, 1 - yh)
    img = ((z * 2 + pair) * 2 + half) * 4 + (x + along) % 4
    txt = (((z + along) % 4 * 2 + pair) * 2 + 1 - half) * 4 + x
    at = jnp.where(yl == 0, img * 4, txt * 4 + 2) if native else jnp.where(yl == 0, txt * 4 + 2, img * 4)
    return codes[pl.ds(at, 1), :] * 64.0 + codes[pl.ds(at + 1, 1), :]


NAT_TILES = (((0,), 0), ((1,), 1), ((2, 3), 2), ((4,), 3))


def slope_kernel(places_of, waits, *refs):
    count = len(places_of)
    scal, places, codes, codes_there = refs[:4]
    row_in, nat_in = refs[4 : 4 + count], refs[4 + count : 9 + count]
    outs = refs[9 + count + waits :]
    slopes, sums = outs[0], outs[1 : 1 + count]
    rows, ids, total = outs[1 + count :]
    start = 0
    for k, (here, along, halves) in enumerate(places_of):
        size = ROWS * len(halves)
        rows[pl.ds(start, size), :] = row_in[k][...]
        for half in halves:
            row = id_row(places, codes if here else codes_there, False, along, half)
            ids[pl.ds(start, ROWS), :] = jnp.broadcast_to(row, (ROWS, ROWS)).T
            start += ROWS
    factor = scal[0] * -LOG2_E
    offset = scal[1] * -LOG2_E

    def nat(tile):
        pieces = [nat_in[k][...] for k in NAT_TILES[tile][0]]
        return pieces[0] if len(pieces) == 1 else jnp.concatenate(pieces, 0)

    def logits(tile):
        return lax.dot_general(rows[...], nat(tile), (((1,), (1,)), ((), ())), preferred_element_type=F32)

    following = logits(0)
    for tile in range(4):
        current = following
        if tile < 3:
            following = logits(tile + 1)
        nat_ids = jnp.concatenate([id_row(places, codes, True, NAT_TILES[tile][1], half) for half in (0, 1)], 1)
        current = factor * current + offset
        match = jnp.concatenate([ids[...], ids[...]], 1) == nat_ids
        part = 1.0 / (1.0 + jnp.exp2(jnp.where(match, -current, current)))
        slope = jnp.where(match, -part, part).astype(BF16)
        slopes[:, pl.ds(tile * TILE, TILE)] = slope
        term = jnp.dot(slope, nat(tile), preferred_element_type=F32)
        if tile == 0:
            total[...] = term
        else:
            total[...] += term
    start = 0
    for k, out in enumerate(sums):
        size = out.shape[0]
        out[...] = total[pl.ds(start, size), :].astype(out.dtype)
        start += size


def slopes_of(scal, places, codes, places_of, rows, nat, after=()):
    whole = sum(r.shape[0] for r in rows)
    got = pl.pallas_call(
        functools.partial(slope_kernel, places_of, len(after)),
        out_shape=[jax.ShapeDtypeStruct((whole, 1024), BF16)]
        + [jax.ShapeDtypeStruct(r.shape, F32 if p[0] else BF16) for r, p in zip(rows, places_of)],
        in_specs=[pl.BlockSpec(memory_space=pltpu.SMEM)] * 2 + [VMEM] * (len(rows) + 7) + [ANYWHERE] * len(after),
        out_specs=[VMEM] * (1 + len(rows)),
        scratch_shapes=[
            pltpu.VMEM((whole, WIDTH), BF16),
            pltpu.VMEM((whole, ROWS), F32),
            pltpu.VMEM((whole, WIDTH), F32),
        ],
        compiler_params=pltpu.CompilerParams(vmem_limit_bytes=SCOPED),
        cost_estimate=pl.CostEstimate(
            flops=4 * whole * 1024 * WIDTH, bytes_accessed=8_000_000, transcendentals=2 * whole * 1024
        ),
    )(scal, places, *codes, *rows, *nat, *after)
    return got[0], got[1:]


def nat_kernel(groups, begins, *refs):
    slopes = refs[: len(groups)]
    row_in = refs[len(groups) : len(groups) + sum(groups)]
    outs = refs[-len(begins) :]
    for begin, out in zip(begins, outs):
        total = None
        first = 0
        for group, count in zip(slopes, groups):
            start = 0
            for k in range(first, first + count):
                size = row_in[k].shape[0]
                term = lax.dot_general(
                    group[pl.ds(start, size), pl.ds(begin, TILE)],
                    row_in[k][...],
                    (((0,), (0,)), ((), ())),
                    preferred_element_type=F32,
                )
                total = term if total is None else total + term
                start += size
            first += count
        out[...] = total.astype(out.dtype)


def nat_sums(slopes, rows, begins, dtypes, after=()):
    groups = tuple(len(r) for r in rows)
    flat = [r for group in rows for r in group]
    return pl.pallas_call(
        functools.partial(nat_kernel, groups, begins),
        out_shape=[jax.ShapeDtypeStruct((TILE, WIDTH), dtype) for dtype in dtypes],
        in_specs=[VMEM] * (len(slopes) + len(flat)) + [ANYWHERE] * len(after),
        out_specs=[VMEM] * len(begins),
        compiler_params=pltpu.CompilerParams(vmem_limit_bytes=SCOPED),
        cost_estimate=pl.CostEstimate(
            flops=1_000_000, bytes_accessed=8_000_000, transcendentals=0
        ),
    )(*slopes, *flat, *after)


def on_device(img_feat, txt_feat, img_map, txt_map, img_label, txt_label, factor, offset):
    z, yh, c, yl, x = (lax.axis_index(a) for a in AXES)
    is_img = yl == 0
    mine, other = spread(c), spread(1 - c)

    feat = jnp.concatenate([img_feat, txt_feat], 0)
    here = to_bf16(feat, mine)
    there = swap(to_bf16(feat, other), "c")
    nat = lambda v: jnp.where(is_img, v[:ROWS], v[ROWS:])
    alt = lambda v: jnp.where(is_img, v[ROWS:], v[:ROWS])
    moved = swap(jnp.concatenate([alt(here), alt(there)], 0), "yl")
    depth_rows = jnp.concatenate([nat(here), moved[:ROWS], nat(there), moved[ROWS:]], 0)

    labels = jnp.stack([img_label, txt_label])
    coded = jnp.stack([labels // 64, labels % 64], 1).astype(BF16).reshape(4, ROWS)
    both = jnp.stack([img_map.reshape(STRIP, 128), txt_map.reshape(STRIP, 128)])
    both = jnp.concatenate([both, jnp.broadcast_to(coded[None], (2, 4, 128)), jnp.zeros((2, 3, 128), BF16)], 1)
    sent = jnp.broadcast_to(both[None, :, None], (8, 2, 4, STRIP + 7, 128)).reshape(64, STRIP + 7, 128)
    got = lax.all_to_all(sent, CHIPS, 0, 0, tiled=True)
    weight = got[:, :STRIP].reshape(HALF, WIDTH)
    codes = got[:, STRIP : STRIP + 4].astype(F32).reshape(256, ROWS)
    codes = (codes, swap(codes, "c"))

    pre = jnp.dot(depth_rows, weight, preferred_element_type=F32)
    pre = pre[:BLOCK] + swap(pre[BLOCK:], "c")
    radius = jnp.sqrt(jnp.sum(pre * pre, axis=1, keepdims=True) + 1e-06)
    unit = pre * (1.0 / radius)
    emb = unit.astype(BF16)

    moved = ring(emb, Y, -1)
    nat = gathered(emb, True)
    own, following, far_a, far_b, previous = gathered(moved, False)
    crossed = lambda values: [swap(v, "c") for v in values]
    rows_own, rows_beside, rows_far = [own], [following, previous], [far_a, far_b]
    rows_own, rows_beside, rows_far = (r + crossed(r) for r in (rows_own, rows_beside, rows_far))

    scal = jnp.concatenate([factor, offset])
    places = jnp.stack([z, yh, yl, x]).astype(jnp.int32)
    both = (0, 1)
    slope_own, (own, own_there) = slopes_of(
        scal, places, codes, ((True, 0, both), (False, 0, both)), rows_own, nat
    )
    slope_beside, (following, previous, following_there, previous_there) = slopes_of(
        scal,
        places,
        codes,
        ((True, 1, both), (True, 3, both), (False, 1, both), (False, 3, both)),
        rows_beside,
        nat,
        (slope_own,),
    )
    slope_far, (far_a, far_b, far_a_there, far_b_there) = slopes_of(
        scal,
        places,
        codes,
        ((True, 2, (0,)), (True, 2, (1,)), (False, 2, (0,)), (False, 2, (1,))),
        rows_far,
        nat,
        (slope_beside,),
    )
    slopes, rows = (slope_own, slope_beside, slope_far), (rows_own, rows_beside, rows_far)
    with_other = lambda mine, there: mine + swap(there, "c").astype(F32)
    far_a = with_other(far_a, far_a_there).astype(BF16)
    far_b = with_other(far_b, far_b_there).astype(BF16)
    (nat_far,) = nat_sums(slopes, rows, (512,), (BF16,), (far_a, far_b))
    nat_own, nat_next, nat_previous = nat_sums(slopes, rows, (0, 256, 768), (F32, BF16, BF16), (nat_far,))

    d_moved, moved_last = reduced(
        [
            with_other(own, own_there),
            with_other(following, following_there).astype(BF16),
            far_a,
            far_b,
            with_other(previous, previous_there).astype(BF16),
        ],
        False,
    )
    nat_parts = [nat_own, nat_next, nat_far[:ROWS], nat_far[ROWS:], nat_previous]
    back = ring(d_moved.astype(BF16), Y, 1)
    d_nat, _ = reduced(nat_parts, True, moved_last)
    grad = factor[0] * (d_nat + back.astype(F32))

    d_pre = ((grad - unit * jnp.sum(unit * grad, axis=1, keepdims=True)) / radius).astype(BF16)
    d_pre = jnp.concatenate([d_pre, swap(d_pre, "c")], 0)
    d_weight = to_bf16(depth_rows, d_pre, ((0,), (0,)))
    sent = d_weight.reshape(64, STRIP, 128)
    late, sent = lax.optimization_barrier((d_pre, sent))
    d_weight = lax.all_to_all(sent, CHIPS, 0, 0, tiled=True)
    d_weight = jnp.sum(d_weight.reshape(8, 2, 4, STRIP, 128).astype(F32), axis=(0, 2))
    d_weight = d_weight.reshape(2, 9, WIDTH)

    d_feat = to_bf16(late, weight, ((1,), (1,)))
    moved = swap(jnp.concatenate([d_feat[ROWS:BLOCK], d_feat[BLOCK + ROWS :]], 0), "yl")
    here = jnp.concatenate([d_feat[:ROWS], moved[:ROWS]], 0)
    there = swap(jnp.concatenate([d_feat[BLOCK : BLOCK + ROWS], moved[ROWS:]], 0), "c")
    d_rows = to_bf16(
        jnp.concatenate([here, there], 1), jnp.concatenate([mine, other], 1), ((1,), (1,))
    )
    nat_grad, alt_grad = d_rows[:ROWS], d_rows[ROWS:]
    img_grad = jnp.where(is_img, nat_grad, alt_grad)
    txt_grad = jnp.where(is_img, alt_grad, nat_grad)
    return (img_grad, txt_grad, d_weight[0], d_weight[1])


def solution(mesh):
    fine = Mesh(mesh.devices.reshape(4, 2, 2, 2, 4), AXES)
    rows = P(AXES, None)
    return jax.shard_map(
        on_device,
        mesh=fine,
        in_specs=(rows, rows, rows, rows, P(AXES), P(AXES), P(), P()),
        out_specs=(rows, rows, rows, rows),
        check_vma=False,
    )
```

```python
import functools

import jax
import jax.numpy as jnp
from jax import lax
from jax.experimental import pallas as pl
from jax.experimental.pallas import tpu as pltpu
from jax.sharding import Mesh, PartitionSpec as P

AXES = ("z", "yh", "c", "yl", "x")
CHIPS = ("z", "yh", "yl", "x")
Y = ("yh", "yl")
ROWS = 128
BLOCK = 256
WIDTH = 1152
HALF = 576
STRIP = 81
BF16 = jnp.bfloat16
F32 = jnp.float32


def ring(value, axes, steps):
    count = lax.axis_size(axes)
    return lax.ppermute(value, axes, [(s, (s + steps) % count) for s in range(count)])


def swap(value, axis):
    return lax.ppermute(value, axis, [(0, 1), (1, 0)])


def spread(core):
    wanted = lax.broadcasted_iota(jnp.int32, (WIDTH, HALF), 1)
    wanted = 144 * (wanted // 72) + 72 * core + wanted % 72
    return (lax.broadcasted_iota(jnp.int32, (WIDTH, HALF), 0) == wanted).astype(BF16)


def to_bf16(a, b, dims=((1,), (0,))):
    return lax.dot_general(a, b, (dims, ((), ())), preferred_element_type=F32).astype(BF16)


def ring_pairs(steps, native):
    pairs = []
    for z in range(4):
        for yl in range(2):
            for x in range(4):
                along_x = (yl == 0) == native
                to = (z, (x + steps) % 4) if along_x else ((z + steps) % 4, x)
                pairs.append(((z * 2 + yl) * 4 + x, (to[0] * 2 + yl) * 4 + to[1]))
    return pairs


def step(value, steps, native):
    return lax.ppermute(value, ("z", "yl", "x"), ring_pairs(steps, native))


def gathered(block, native):
    previous = step(block, 1, native)
    following = step(block, -1, native)
    far_a = step(previous[:ROWS], 1, native)
    far_b = step(following[ROWS:], -1, native)
    return [block, following, far_a, far_b, previous]


def added_half(whole, half, first):
    low, high = whole[:ROWS], whole[ROWS:]
    if first:
        low = (low.astype(F32) + half.astype(F32)).astype(BF16)
    else:
        high = (high.astype(F32) + half.astype(F32)).astype(BF16)
    return jnp.concatenate([low, high], 0)


def reduced(parts, native, first=None):
    own, following, far_a, far_b, previous = parts
    late = step(far_a, -1, native), step(far_b, 1, native)
    if first is not None:
        late = lax.optimization_barrier((*late, *first))
    previous = added_half(previous, late[0], True)
    following = added_half(following, late[1], False)
    from_next = step(previous, -1, native)
    from_previous = step(following, 1, native)
    return own.astype(F32) + from_next.astype(F32) + from_previous.astype(F32), (previous, following)


TILE = 256
SCOPED = 13 * 1024 * 1024
LOG2_E = 1.4426950408889634
VMEM = pl.BlockSpec(memory_space=pltpu.VMEM)
ANYWHERE = pl.BlockSpec(memory_space=pl.ANY)


def id_row(places, codes, native, along, half):
    z, yh, yl, x = (places[k] for k in range(4))
    pair = yh if native else jnp.where(yl == 0, yh, 1 - yh)
    img = ((z * 2 + pair) * 2 + half) * 4 + (x + along) % 4
    txt = (((z + along) % 4 * 2 + pair) * 2 + 1 - half) * 4 + x
    at = jnp.where(yl == 0, img * 4, txt * 4 + 2) if native else jnp.where(yl == 0, txt * 4 + 2, img * 4)
    return codes[pl.ds(at, 1), :] * 64.0 + codes[pl.ds(at + 1, 1), :]


NAT_TILES = (((0,), 0), ((1,), 1), ((2, 3), 2), ((4,), 3))


def slope_kernel(places_of, waits, *refs):
    count = len(places_of)
    scal, places, codes, codes_there = refs[:4]
    row_in, nat_in = refs[4 : 4 + count], refs[4 + count : 9 + count]
    outs = refs[9 + count + waits :]
    slopes, sums = outs[0], outs[1 : 1 + count]
    rows, ids, total = outs[1 + count :]
    start = 0
    for k, (here, along, halves) in enumerate(places_of):
        size = ROWS * len(halves)
        rows[pl.ds(start, size), :] = row_in[k][...]
        for half in halves:
            row = id_row(places, codes if here else codes_there, False, along, half)
            ids[pl.ds(start, ROWS), :] = jnp.broadcast_to(row, (ROWS, ROWS)).T
            start += ROWS
    factor = scal[0] * -LOG2_E
    offset = scal[1] * -LOG2_E

    def nat(tile):
        pieces = [nat_in[k][...] for k in NAT_TILES[tile][0]]
        return pieces[0] if len(pieces) == 1 else jnp.concatenate(pieces, 0)

    def logits(tile):
        return lax.dot_general(rows[...], nat(tile), (((1,), (1,)), ((), ())), preferred_element_type=F32)

    following = logits(0)
    for tile in range(4):
        current = following
        if tile < 3:
            following = logits(tile + 1)
        nat_ids = jnp.concatenate([id_row(places, codes, True, NAT_TILES[tile][1], half) for half in (0, 1)], 1)
        current = factor * current + offset
        match = jnp.concatenate([ids[...], ids[...]], 1) == nat_ids
        part = 1.0 / (1.0 + jnp.exp2(jnp.where(match, -current, current)))
        slope = jnp.where(match, -part, part).astype(BF16)
        slopes[:, pl.ds(tile * TILE, TILE)] = slope
        term = jnp.dot(slope, nat(tile), preferred_element_type=F32)
        if tile == 0:
            total[...] = term
        else:
            total[...] += term
    start = 0
    for k, out in enumerate(sums):
        size = out.shape[0]
        out[...] = total[pl.ds(start, size), :].astype(out.dtype)
        start += size


def slopes_of(scal, places, codes, places_of, rows, nat, after=()):
    whole = sum(r.shape[0] for r in rows)
    got = pl.pallas_call(
        functools.partial(slope_kernel, places_of, len(after)),
        out_shape=[jax.ShapeDtypeStruct((whole, 1024), BF16)]
        + [jax.ShapeDtypeStruct(r.shape, F32 if p[0] else BF16) for r, p in zip(rows, places_of)],
        in_specs=[pl.BlockSpec(memory_space=pltpu.SMEM)] * 2 + [VMEM] * (len(rows) + 7) + [ANYWHERE] * len(after),
        out_specs=[VMEM] * (1 + len(rows)),
        scratch_shapes=[
            pltpu.VMEM((whole, WIDTH), BF16),
            pltpu.VMEM((whole, ROWS), F32),
            pltpu.VMEM((whole, WIDTH), F32),
        ],
        compiler_params=pltpu.CompilerParams(vmem_limit_bytes=SCOPED),
        cost_estimate=pl.CostEstimate(
            flops=4 * whole * 1024 * WIDTH, bytes_accessed=8_000_000, transcendentals=2 * whole * 1024
        ),
    )(scal, places, *codes, *rows, *nat, *after)
    return got[0], got[1:]


def nat_kernel(groups, begins, *refs):
    slopes = refs[: len(groups)]
    row_in = refs[len(groups) : len(groups) + sum(groups)]
    outs = refs[-len(begins) :]
    for begin, out in zip(begins, outs):
        total = None
        first = 0
        for group, count in zip(slopes, groups):
            start = 0
            for k in range(first, first + count):
                size = row_in[k].shape[0]
                term = lax.dot_general(
                    group[pl.ds(start, size), pl.ds(begin, TILE)],
                    row_in[k][...],
                    (((0,), (0,)), ((), ())),
                    preferred_element_type=F32,
                )
                total = term if total is None else total + term
                start += size
            first += count
        out[...] = total.astype(out.dtype)


def nat_sums(slopes, rows, begins, dtypes, after=()):
    groups = tuple(len(r) for r in rows)
    flat = [r for group in rows for r in group]
    return pl.pallas_call(
        functools.partial(nat_kernel, groups, begins),
        out_shape=[jax.ShapeDtypeStruct((TILE, WIDTH), dtype) for dtype in dtypes],
        in_specs=[VMEM] * (len(slopes) + len(flat)) + [ANYWHERE] * len(after),
        out_specs=[VMEM] * len(begins),
        compiler_params=pltpu.CompilerParams(vmem_limit_bytes=SCOPED),
        cost_estimate=pl.CostEstimate(
            flops=1_000_000, bytes_accessed=8_000_000, transcendentals=0
        ),
    )(*slopes, *flat, *after)


def on_device(img_feat, txt_feat, img_map, txt_map, img_label, txt_label, factor, offset):
    z, yh, c, yl, x = (lax.axis_index(a) for a in AXES)
    is_img = yl == 0
    mine, other = spread(c), spread(1 - c)

    feat = jnp.concatenate([img_feat, txt_feat], 0)
    here = to_bf16(feat, mine)
    there = swap(to_bf16(feat, other), "c")
    nat = lambda v: jnp.where(is_img, v[:ROWS], v[ROWS:])
    alt = lambda v: jnp.where(is_img, v[ROWS:], v[:ROWS])
    moved = swap(jnp.concatenate([alt(here), alt(there)], 0), "yl")
    depth_rows = jnp.concatenate([nat(here), moved[:ROWS], nat(there), moved[ROWS:]], 0)

    labels = jnp.stack([img_label, txt_label])
    coded = jnp.stack([labels // 64, labels % 64], 1).astype(BF16).reshape(4, ROWS)
    both = jnp.stack([img_map.reshape(STRIP, 128), txt_map.reshape(STRIP, 128)])
    both = jnp.concatenate([both, jnp.broadcast_to(coded[None], (2, 4, 128)), jnp.zeros((2, 3, 128), BF16)], 1)
    sent = jnp.broadcast_to(both[None, :, None], (8, 2, 4, STRIP + 7, 128)).reshape(64, STRIP + 7, 128)
    got = lax.all_to_all(sent, CHIPS, 0, 0, tiled=True)
    weight = got[:, :STRIP].reshape(HALF, WIDTH)
    codes = got[:, STRIP : STRIP + 4].astype(F32).reshape(256, ROWS)
    codes = (codes, swap(codes, "c"))

    pre = jnp.dot(depth_rows, weight, preferred_element_type=F32)
    pre = pre[:BLOCK] + swap(pre[BLOCK:].astype(BF16), "c").astype(F32)
    radius = jnp.sqrt(jnp.sum(pre * pre, axis=1, keepdims=True) + 1e-06)
    unit = pre * (1.0 / radius)
    emb = unit.astype(BF16)

    moved = ring(emb, Y, -1)
    nat = gathered(emb, True)
    own, following, far_a, far_b, previous = gathered(moved, False)
    crossed = lambda values: [swap(v, "c") for v in values]
    rows_own, rows_beside, rows_far = [own], [following, previous], [far_a, far_b]
    rows_own, rows_beside, rows_far = (r + crossed(r) for r in (rows_own, rows_beside, rows_far))

    scal = jnp.concatenate([factor, offset])
    places = jnp.stack([z, yh, yl, x]).astype(jnp.int32)
    both = (0, 1)
    slope_own, (own, own_there) = slopes_of(
        scal, places, codes, ((True, 0, both), (False, 0, both)), rows_own, nat
    )
    slope_beside, (following, previous, following_there, previous_there) = slopes_of(
        scal,
        places,
        codes,
        ((True, 1, both), (True, 3, both), (False, 1, both), (False, 3, both)),
        rows_beside,
        nat,
        (slope_own,),
    )
    slope_far, (far_a, far_b, far_a_there, far_b_there) = slopes_of(
        scal,
        places,
        codes,
        ((True, 2, (0,)), (True, 2, (1,)), (False, 2, (0,)), (False, 2, (1,))),
        rows_far,
        nat,
        (slope_beside,),
    )
    slopes, rows = (slope_own, slope_beside, slope_far), (rows_own, rows_beside, rows_far)
    with_other = lambda mine, there: mine + swap(there, "c").astype(F32)
    far_a = with_other(far_a, far_a_there).astype(BF16)
    far_b = with_other(far_b, far_b_there).astype(BF16)
    (nat_far,) = nat_sums(slopes, rows, (512,), (BF16,), (far_a, far_b))
    nat_own, nat_next, nat_previous = nat_sums(slopes, rows, (0, 256, 768), (F32, BF16, BF16), (nat_far,))

    d_moved, moved_last = reduced(
        [
            with_other(own, own_there),
            with_other(following, following_there).astype(BF16),
            far_a,
            far_b,
            with_other(previous, previous_there).astype(BF16),
        ],
        False,
    )
    nat_parts = [nat_own, nat_next, nat_far[:ROWS], nat_far[ROWS:], nat_previous]
    back = ring(d_moved.astype(BF16), Y, 1)
    d_nat, _ = reduced(nat_parts, True, moved_last)
    grad = factor[0] * (d_nat + back.astype(F32))

    d_pre = ((grad - unit * jnp.sum(unit * grad, axis=1, keepdims=True)) / radius).astype(BF16)
    d_pre = jnp.concatenate([d_pre, swap(d_pre, "c")], 0)
    d_weight = to_bf16(depth_rows, d_pre, ((0,), (0,)))
    sent = d_weight.reshape(64, STRIP, 128)
    late, sent = lax.optimization_barrier((d_pre, sent))
    d_weight = lax.all_to_all(sent, CHIPS, 0, 0, tiled=True)
    d_weight = jnp.sum(d_weight.reshape(8, 2, 4, STRIP, 128).astype(F32), axis=(0, 2))
    d_weight = d_weight.reshape(2, 9, WIDTH)

    d_feat = to_bf16(late, weight, ((1,), (1,)))
    moved = swap(jnp.concatenate([d_feat[ROWS:BLOCK], d_feat[BLOCK + ROWS :]], 0), "yl")
    here = jnp.concatenate([d_feat[:ROWS], moved[:ROWS]], 0)
    there = swap(jnp.concatenate([d_feat[BLOCK : BLOCK + ROWS], moved[ROWS:]], 0), "c")
    d_rows = to_bf16(
        jnp.concatenate([here, there], 1), jnp.concatenate([mine, other], 1), ((1,), (1,))
    )
    nat_grad, alt_grad = d_rows[:ROWS], d_rows[ROWS:]
    img_grad = jnp.where(is_img, nat_grad, alt_grad)
    txt_grad = jnp.where(is_img, alt_grad, nat_grad)
    return (img_grad, txt_grad, d_weight[0], d_weight[1])


def solution(mesh):
    fine = Mesh(mesh.devices.reshape(4, 2, 2, 2, 4), AXES)
    rows = P(AXES, None)
    return jax.shard_map(
        on_device,
        mesh=fine,
        in_specs=(rows, rows, rows, rows, P(AXES), P(AXES), P(), P()),
        out_specs=(rows, rows, rows, rows),
        check_vma=False,
    )
```
